128 devices in a mesh: ctx: 32 (over z, x, core), head: 4 (over y).
Axes of the slice: x: 4, y: 4, z: 4, core: 2. Of those that a mesh axis runs over, the one named last changes fastest.
Arguments:
- queries: bfloat16 [32768, 4096], P('ctx', 'head'), may hold values from -12 to 12
- keys: bfloat16 [32768, 4096], P('ctx', 'head'), may hold values from -9 to 9
- values: bfloat16 [32768, 4096], P('ctx', 'head'), may hold values from -6 to 6
- w_out: bfloat16 [4096, 4096], P('head'), may hold values from -0.125 to 0.125
Outputs:
- mixed: bfloat16 [32768, 4096], P('ctx', 'head')
The draws below stay inside these ranges and needn't reach their ends.
All inputs are finite; a program needn't handle non-finite values.
Results may differ from the reference program's by a relative error of at most 0.013.
Values may be sent and summed in bfloat16 or wider, within the bound.
A program may use at most 192 MiB of HBM per device.

```python
import jax
import jax.numpy as jnp
from jax import lax

HEADS = 32
DH = 128
D = 4096
S_DEV = 1024
R_MID = 8
R_TOP = 32
G_MID = 8
TOKENS = 32768
HEADS_DEV = 8


def draw_queries(key, part):
    mine = jax.random.fold_in(key, 11)
    base = 3.0 * jnp.clip(jax.random.normal(mine, (TOKENS, HEADS * DH), jnp.float32), -4.0, 4.0)
    return base.astype(jnp.bfloat16)


def draw_keys(key, part):
    mine = jax.random.fold_in(key, 23)
    base = jnp.clip(jax.random.normal(mine, (TOKENS, HEADS * DH), jnp.float32), -6.0, 6.0)
    return base.astype(jnp.bfloat16)


def spiked(values, stream_key, source, target, shards_of, factor):
    def block_of(axis_at):
        return (jnp.arange(values.shape[axis_at]) // (values.shape[axis_at] // shards_of)).reshape((-1,) + (1,) * (values.ndim - 1 - axis_at))

    one_side = jax.random.permutation(stream_key, shards_of)[block_of(target)]
    second = (block_of(target) + shards_of // 2) % shards_of
    return jnp.where((block_of(source) == one_side) | (block_of(source) == second), factor * values, values)


def block_scale(own_key, extent, shards, smallest, top_value):
    gain = 1.0
    for dim, blocks in shards:
        heights = jax.random.uniform(jax.random.fold_in(jax.random.fold_in(own_key, 6), dim), (blocks,), jnp.float32, smallest / len(shards), top_value / len(shards))
        gain = gain * jnp.repeat(jnp.exp(heights), extent[dim] // blocks).reshape((-1,) + (1,) * (len(extent) - 1 - dim))
    return gain


def centred(key, shape, spread, reach, cuts=(), held_as=jnp.bfloat16):
    level = block_scale(key, shape, cuts, -0.22, 0.18) if cuts else 1.0
    values = jax.random.normal(key, shape, jnp.float32) * spread * level
    return jnp.minimum(jnp.maximum(values, -reach), reach).astype(held_as)


def heavy_noise(stream_key, dims, spread, bound, pieces, heavy, kind=jnp.bfloat16):
    array = spread * jax.random.normal(stream_key, dims, jnp.float32)
    if pieces:
        array = array * block_scale(stream_key, dims, pieces, -0.22, 0.18)
    return jnp.clip(spiked(array, jax.random.fold_in(stream_key, 3), *heavy), -bound, bound).astype(kind)


def setup_inputs(seed: int = 0) -> dict:
    seeds = jax.random.split(jax.random.key(seed), 5)
    return {
        "queries": draw_queries(jax.random.fold_in(seeds[4], 71), 0),
        "keys": draw_keys(jax.random.fold_in(seeds[4], 71), 0),
        "values": centred(seeds[2], (TOKENS, D), 1.0, 6.0, ((0, 32), (1, 4))),
        "w_out": heavy_noise(seeds[3], (D, D), D ** -0.5, 0.125, ((0, 4),), (0, 1, 4, 2.0)),
    }


BIG_NEG = -1e30


def ref_stats(qs, ks, vs):
    count = qs.shape[1]
    scores = jnp.einsum("sqd,skd->sqk", qs, ks) * (DH ** -0.5)
    lower = jnp.arange(count, dtype=jnp.int32)[None, :] <= jnp.arange(count, dtype=jnp.int32)[:, None]
    scores = jnp.where(lower[None], scores, BIG_NEG)
    peak = jnp.max(scores, axis=2)
    expo = jnp.exp(scores - peak[:, :, None])
    total = jnp.sum(expo, axis=2)
    weights = lax.optimization_barrier(expo.astype(jnp.bfloat16)).astype(jnp.float32)
    numer = jnp.einsum("sqk,skd->sqd", weights, vs)
    return peak.reshape(-1), total.reshape(-1), numer.reshape(-1, DH)


def pick_rows(field, stride, offset):
    view = field.reshape(TOKENS // stride, stride, DH)
    return lax.dynamic_index_in_dim(view, offset, 1, keepdims=False)


def expand(field, stride, offset, fill):
    hit = jnp.arange(stride, dtype=jnp.int32) == offset
    if field.ndim == 2:
        spread_out = jnp.where(hit[None, :, None], field[:, None, :], fill)
    else:
        spread_out = jnp.where(hit[None, :], field[:, None], fill)
    return spread_out.reshape((TOKENS,) + field.shape[1:])


def reference(queries, keys, values, w_out):
    mid_len = G_MID * S_DEV // R_MID

    def one_head(index):
        qh = lax.dynamic_slice_in_dim(queries, index * DH, DH, 1).astype(jnp.float32)
        kh = lax.dynamic_slice_in_dim(keys, index * DH, DH, 1).astype(jnp.float32)
        vh = lax.dynamic_slice_in_dim(values, index * DH, DH, 1).astype(jnp.float32)
        mid_off = index % R_MID
        top_off = index % R_TOP
        shape0 = (TOKENS // S_DEV, S_DEV, DH)
        peak0, total0, numer0 = ref_stats(qh.reshape(shape0), kh.reshape(shape0), vh.reshape(shape0))
        shape1 = (TOKENS // (G_MID * S_DEV), mid_len, DH)
        peak1, total1, numer1 = ref_stats(pick_rows(qh, R_MID, mid_off).reshape(shape1),
                                          pick_rows(kh, R_MID, mid_off).reshape(shape1),
                                          pick_rows(vh, R_MID, mid_off).reshape(shape1))
        peak2, total2, numer2 = ref_stats(pick_rows(qh, R_TOP, top_off)[None],
                                          pick_rows(kh, R_TOP, top_off)[None],
                                          pick_rows(vh, R_TOP, top_off)[None])
        peak1 = expand(peak1, R_MID, mid_off, BIG_NEG)
        total1 = expand(total1, R_MID, mid_off, 0.0)
        numer1 = expand(numer1, R_MID, mid_off, 0.0)
        peak2 = expand(peak2, R_TOP, top_off, BIG_NEG)
        total2 = expand(total2, R_TOP, top_off, 0.0)
        numer2 = expand(numer2, R_TOP, top_off, 0.0)
        top = jnp.maximum(peak0, jnp.maximum(peak1, peak2))
        fac0 = jnp.exp(peak0 - top)
        fac1 = jnp.exp(peak1 - top)
        fac2 = jnp.exp(peak2 - top)
        upper = numer0 * fac0[:, None] + numer1 * fac1[:, None] + numer2 * fac2[:, None]
        lower_sum = total0 * fac0 + total1 * fac1 + total2 * fac2
        return (upper / lower_sum[:, None]).astype(jnp.bfloat16)

    stacked = lax.map(one_head, jnp.arange(HEADS, dtype=jnp.int32))
    attn = stacked.transpose(1, 0, 2).reshape(TOKENS, HEADS * DH)
    group = HEADS_DEV * DH
    mixed = jnp.zeros((TOKENS, HEADS * DH), jnp.float32)
    for index in range(HEADS // HEADS_DEV):
        left = attn[:, index * group:(index + 1) * group].astype(jnp.float32)
        right = w_out[index * group:(index + 1) * group, :].astype(jnp.float32)
        partial_sum = jnp.dot(left, right, precision=lax.Precision.HIGHEST)
        mixed = mixed + lax.optimization_barrier(partial_sum.astype(jnp.bfloat16)).astype(jnp.float32)
    return mixed.astype(jnp.bfloat16)
```

```python
import math

import jax
import jax.numpy as jnp
from jax import lax
from jax.experimental import pallas as pl
from jax.experimental.pallas import tpu as pltpu
from jax.sharding import PartitionSpec as P

MESH = pl.DeviceIdType.MESH
DH = 128
HEADS_HERE = 8
ROWS = 1024
COLS = 1024
MID = 128
TOP = 32
R_MID = 8
R_TOP = 32
QB = 256
NEG = -1e30
COEF = DH ** -0.5 / math.log(2.0)
F32 = jnp.float32
BF16 = jnp.bfloat16


def dot_t(a, b):
    return lax.dot_general(a, b, (((1,), (1,)), ((), ())), preferred_element_type=F32)


def dot(a, b):
    return jnp.dot(a, b, preferred_element_type=F32)


class Ring:
    def __init__(self, copy, plus, minus, own, far_plus, far_minus):
        self.first = [copy(*own[0], plus), copy(*own[1], minus)]
        self.second = [copy(*far_plus, plus), copy(*far_minus, minus)]

    def start(self):
        for one in self.first:
            one.start()

    def forward(self):
        for came, onward in zip(self.first, self.second):
            came.wait_recv()
            onward.start()

    def finish(self):
        for one in self.second:
            one.wait_recv()

    def drain(self):
        for one in self.first + self.second:
            one.wait_send()


def body(q_hbm, k_hbm, v_hbm, w_hbm, out_hbm,
         q, k, v, wc_own, wo_own, attn, attn_p, mid, top, wc, wo, rs_s, rs_r, out,
         patch, patch_p, qa, qt, wide, m0, l0, n0, aff, tops, send, recv, lsem):
    place = lax.axis_index("ctx")
    h = lax.axis_index("head")
    z = lax.div(place, 8)
    x = lax.rem(lax.div(place, 2), 4)
    c = lax.rem(place, 2)
    near = h + 1 - 2 * lax.rem(h, 2)
    pair = (1 - c) * near + c * (3 - h)
    cross = c * near + (1 - c) * (3 - h)
    diag = lax.rem(h + 2, 4)

    def at(zz, xx, cc):
        return lax.rem(zz, 4) * 8 + lax.rem(xx, 4) * 2 + cc

    xp, xm = (at(z, x + 1, c), h), (at(z, x + 3, c), h)
    zp, zm = (at(z + 1, x, c), h), (at(z + 3, x, c), h)
    sib = (at(z, x, 1 - c), h)
    dp, dc = (place, pair), (place, cross)

    count = [0]

    def copy(src, dst, device):
        i = count[0]
        count[0] += 1
        return pltpu.make_async_remote_copy(
            src_ref=src, dst_ref=dst, send_sem=send.at[i], recv_sem=recv.at[i],
            device_id=device, device_id_type=MESH)

    lcount = [0]

    def load(src, dst):
        i = lcount[0]
        lcount[0] += 1
        return pltpu.make_async_copy(src, dst, lsem.at[i])

    xl, xr = lax.rem(x + 3, 4), lax.rem(x + 1, 4)

    k_load, v_load, q_load = load(k_hbm, k), load(v_hbm, v), load(q_hbm, q)
    for one in (k_load, v_load, q_load):
        one.start()

    barrier = pltpu.get_barrier_semaphore()
    for other in (xp, xm, zp, zm, sib, dp, dc):
        pl.semaphore_signal(barrier, inc=1, device_id=other, device_id_type=MESH)
    pl.semaphore_wait(barrier, 7)

    def w_piece(block):
        return w_hbm.at[pl.ds(pl.multiple_of(x * 256, 256), 256),
                        pl.ds(pl.multiple_of(block * COLS + z * 256, 256), 256)]

    wc_hop = copy(w_piece(diag), wc.at[0, x], dp)
    wo_hop = copy(w_piece(pair), wo.at[x, 0], dp)
    wc_hop.start()
    wo_hop.start()

    wc_x = Ring(copy, xp, xm,
                [(wc.at[0, x], wc.at[0, x])] * 2,
                (wc.at[0, xl, pl.ds(0, 128)], wc.at[0, xl, pl.ds(0, 128)]),
                (wc.at[0, xr, pl.ds(128, 128)], wc.at[0, xr, pl.ds(128, 128)]))
    wc_z = Ring(copy, zp, zm,
                [(wc.at[0], wc.at[3]), (wc.at[0], wc.at[1])],
                (wc.at[3, pl.ds(0, 2)], wc.at[2, pl.ds(0, 2)]),
                (wc.at[1, pl.ds(2, 2)], wc.at[2, pl.ds(2, 2)]))
    wo_z = Ring(copy, zp, zm,
                [(wo.at[x, 0], wo.at[x, 3]), (wo.at[x, 0], wo.at[x, 1])],
                (wo.at[x, 3, pl.ds(0, 128)], wo.at[x, 2, pl.ds(0, 128)]),
                (wo.at[x, 1, pl.ds(128, 128)], wo.at[x, 2, pl.ds(128, 128)]))
    wo_x = Ring(copy, xp, xm,
                [(wo.at[x], wo.at[x])] * 2,
                (wo.at[xl, pl.ds(0, 2)], wo.at[xl, pl.ds(0, 2)]),
                (wo.at[xr, pl.ds(2, 2)], wo.at[xr, pl.ds(2, 2)]))
    mid_x = Ring(copy, xp, xm,
                 [(mid.at[x, c], mid.at[x, c])] * 2,
                 (mid.at[xl, c, 0], mid.at[xl, c, 0]),
                 (mid.at[xr, c, 1], mid.at[xr, c, 1]))
    top_x = Ring(copy, xp, xm,
                 [(top.at[0, c, x], top.at[0, c, x])] * 2,
                 (top.at[0, c, xl, 0], top.at[0, c, xl, 0]),
                 (top.at[0, c, xr, 1], top.at[0, c, xr, 1]))
    top_z = Ring(copy, zp, zm,
                 [(top.at[0, c], top.at[3, c]), (top.at[0, c], top.at[1, c])],
                 (top.at[3, c, pl.ds(0, 2)], top.at[2, c, pl.ds(0, 2)]),
                 (top.at[1, c, pl.ds(2, 2)], top.at[2, c, pl.ds(2, 2)]))
    mid_sib = [copy(mid.at[lax.rem(x + d, 4), c], mid.at[lax.rem(x + d, 4), c], sib) for d in range(4)]
    top_sib = [copy(top.at[d, c], top.at[d, c], sib) for d in range(4)]

    def select(src, cols, j):
        wide[...] = src[:, cols].astype(F32)
        rows = wide[pl.ds(j, MID, stride=R_MID), :]
        few = wide[pl.ds(h * 8 + j, TOP, stride=R_TOP), :]
        return rows.astype(BF16), few.astype(BF16)

    def pick(j, carry):
        cols = pl.ds(pl.multiple_of(j * DH, DH), DH)
        for kv, src in enumerate((k, v)):
            rows, few = select(src, cols, j)
            mid[x, c, kv, j] = rows
            top[0, c, x, kv, j] = few
        return carry

    k_load.wait()
    v_load.wait()
    lax.fori_loop(0, HEADS_HERE, pick, 0)
    top_x.start()
    mid_x.start()
    mid_sib[0].start()

    w_loads = []
    for d in range(4):
        zc = lax.rem(z + d, 4) * 256
        for block, dst in ((cross, wc_own), (h, wo_own)):
            w_loads.append(load(w_hbm.at[:, pl.ds(pl.multiple_of(block * COLS + zc, 256), 256)], dst.at[d]))
    for one in w_loads:
        one.start()

    base = count[0]
    count[0] += HEADS_HERE
    tri = lax.broadcasted_iota(jnp.int32, (QB, QB), 0) >= lax.broadcasted_iota(jnp.int32, (QB, QB), 1)

    def attn_send(j):
        cols = pl.ds(pl.multiple_of(j * DH, DH), DH)
        return pltpu.make_async_remote_copy(
            src_ref=attn.at[:, cols], dst_ref=attn_p.at[:, cols],
            send_sem=send.at[base + j], recv_sem=recv.at[base + j],
            device_id=dp, device_id_type=MESH)

    def level0(j, carry):
        cols = pl.ds(pl.multiple_of(j * DH, DH), DH)
        rows, few = select(q, cols, j)
        qa[j] = rows
        qt[j] = few
        vx = jnp.concatenate([v[:, cols], jnp.ones((ROWS, DH), BF16)], axis=1)
        for i in range(ROWS // QB):
            here = pl.ds(i * QB, QB)
            qi = q[here, cols]
            s_d = jnp.where(tri, dot_t(qi, k[here, cols]), NEG)
            peak = jnp.max(s_d, axis=1, keepdims=True)
            if i:
                s_o = dot_t(qi, k[pl.ds(0, i * QB), cols])
                peak = jnp.maximum(peak, jnp.max(s_o, axis=1, keepdims=True))
            p_d = jnp.exp2((s_d - peak) * COEF).astype(BF16)
            acc = dot(p_d, vx[i * QB:(i + 1) * QB])
            if i:
                p_o = jnp.exp2((s_o - peak) * COEF).astype(BF16)
                acc = acc + dot(p_o, vx[:i * QB])
            numer, total = acc[:, :DH], acc[:, DH:]
            m0[here] = jnp.broadcast_to(peak, (QB, DH))
            n0[here] = numer
            l0[here] = total
            attn[here, cols] = (numer / total).astype(BF16)
        picked = pl.ds(j, MID, stride=R_MID)
        aff[j, 0] = m0[picked, :]
        aff[j, 1] = l0[picked, :]
        aff[j, 2] = n0[picked, :]
        attn_send(j).start()
        return carry

    q_load.wait()
    lax.fori_loop(0, 2, level0, 0)
    wc_hop.wait_recv()
    wo_hop.wait_recv()
    wc_x.start()
    wo_z.start()
    top_x.forward()
    lax.fori_loop(2, 5, level0, 0)
    top_x.finish()
    top_z.start()
    top_sib[0].start()
    lax.fori_loop(5, 8, level0, 0)
    mid_x.forward()
    mid_sib[1].start()
    mid_sib[3].start()
    wc_x.forward()
    wo_z.forward()
    mid_x.finish()
    mid_sib[2].start()
    wc_x.finish()
    wc_z.start()
    top_z.forward()
    top_sib[1].start()
    top_sib[3].start()
    wo_z.finish()
    wo_x.start()
    top_z.finish()
    top_sib[2].start()
    for one in mid_sib + top_sib:
        one.wait_recv()

    def late(j, carry):
        def attend(qs, key, val, ok):
            s = jnp.where(ok, dot_t(qs, key), NEG)
            peak = jnp.max(s, axis=1, keepdims=True)
            p = jnp.exp2((s - peak) * COEF).astype(BF16)
            acc = dot(p, jnp.concatenate([val, jnp.ones((1024, DH), BF16)], axis=1))
            return jnp.broadcast_to(peak, (qs.shape[0], DH)), acc[:, DH:], acc[:, :DH]

        row = lax.broadcasted_iota(jnp.int32, (MID, 1024), 0)
        col = lax.broadcasted_iota(jnp.int32, (MID, 1024), 1)
        m1, l1, n1 = attend(qa[j], mid[:, :, 0, j].reshape(1024, DH), mid[:, :, 1, j].reshape(1024, DH),
                            col <= row + (x * 2 + c) * MID)
        row = lax.broadcasted_iota(jnp.int32, (TOP, 1024), 0)
        col = lax.broadcasted_iota(jnp.int32, (TOP, 1024), 1)
        kz = (z + (col >> 8)) & 3
        spot = ((kz * 8 + ((col >> 5) & 3) * 2 + ((col >> 7) & 1)) * TOP) + (col & 31)
        m2, l2, n2 = attend(qt[j], top[:, :, :, 0, j].reshape(1024, DH), top[:, :, :, 1, j].reshape(1024, DH),
                            spot <= row + place * TOP)
        tops[0] = jnp.full((MID, DH), NEG, F32)
        tops[1] = jnp.zeros((MID, DH), F32)
        tops[2] = jnp.zeros((MID, DH), F32)
        hit = pl.ds(h, TOP, stride=4)
        tops[0, hit, :] = m2
        tops[1, hit, :] = l2
        tops[2, hit, :] = n2
        ma, mt = aff[j, 0], tops[0]
        peak = jnp.maximum(ma, jnp.maximum(m1, mt))
        fa = jnp.exp2((ma - peak) * COEF)
        fm = jnp.exp2((m1 - peak) * COEF)
        ft = jnp.exp2((mt - peak) * COEF)
        upper = aff[j, 2] * fa + n1 * fm + tops[2] * ft
        lower = aff[j, 1] * fa + l1 * fm + tops[1] * ft
        patch[j] = (upper / lower).astype(BF16)
        return carry

    lax.fori_loop(0, HEADS_HERE, late, 0)
    patch_send = copy(patch, patch_p, dp)
    patch_send.start()

    def mend(target, source):
        def one(j, carry):
            cols = pl.ds(pl.multiple_of(j * DH, DH), DH)
            old = target[:, cols].astype(F32).reshape(MID, R_MID, DH)
            new = source[j].astype(F32).reshape(MID, 1, DH)
            lane = lax.broadcasted_iota(jnp.int32, (MID, R_MID, DH), 1)
            target[:, cols] = jnp.where(lane == j, new, old).reshape(ROWS, DH).astype(BF16)
            return carry
        lax.fori_loop(0, HEADS_HERE, one, 0)

    for j in range(HEADS_HERE):
        attn_send(j).wait_send()
    mend(attn, patch)
    wc_z.forward()
    wo_x.forward()
    for j in range(HEADS_HERE):
        attn_send(j).wait_recv()
    patch_send.wait_recv()
    mend(attn_p, patch_p)

    for one in w_loads:
        one.wait()
    HALF = ROWS // 2
    sums = []
    for d in (0, 1, 3, 2):
        if d == 2:
            wc_z.finish()
        for part in range(2):
            here = pl.ds(part * HALF, HALF)
            rs_s[d, here] = (dot(attn[here], wc_own[d])
                             + dot(attn_p[here], wc[d].reshape(1024, 256))).astype(BF16)
            one = copy(rs_s.at[d, here], rs_r.at[d, here], dc)
            one.start()
            sums.append((d, here, one))
    wo_x.finish()
    stores = []
    for d, here, one in sums:
        mine = dot(attn[here], wo_own[d]) + dot(attn_p[here], wo[:, d].reshape(1024, 256))
        one.wait_recv()
        out[d, here] = (mine + rs_r[d, here].astype(F32)).astype(BF16)
        zc = pl.multiple_of(lax.rem(z + d, 4) * 256, 256)
        stores.append(load(out.at[d, here], out_hbm.at[here, pl.ds(zc, 256)]))
        stores[-1].start()

    for ring in (wc_x, wc_z, wo_z, wo_x, mid_x, top_x, top_z):
        ring.drain()
    for one in mid_sib + top_sib + [wc_hop, wo_hop, patch_send] + [s[2] for s in sums]:
        one.wait_send()
    for one in stores:
        one.wait()


def local(queries, keys, values, w_out):
    any_space = pl.BlockSpec(memory_space=pl.ANY)
    vm = pltpu.VMEM
    return pl.pallas_call(
        body,
        name="attend",
        out_shape=jax.ShapeDtypeStruct((ROWS, COLS), BF16),
        in_specs=[any_space] * 4,
        out_specs=any_space,
        scratch_shapes=[
            vm((ROWS, COLS), BF16), vm((ROWS, COLS), BF16), vm((ROWS, COLS), BF16),
            vm((4, 1024, 256), BF16), vm((4, 1024, 256), BF16),
            vm((ROWS, COLS), BF16), vm((ROWS, COLS), BF16),
            vm((4, 2, 2, 8, MID, DH), BF16),
            vm((4, 2, 4, 2, 8, TOP, DH), BF16),
            vm((4, 4, 256, 256), BF16), vm((4, 4, 256, 256), BF16),
            vm((4, ROWS, 256), BF16), vm((4, ROWS, 256), BF16), vm((4, ROWS, 256), BF16),
            vm((8, MID, DH), BF16), vm((8, MID, DH), BF16),
            vm((8, MID, DH), BF16), vm((8, TOP, DH), BF16),
            vm((ROWS, DH), F32), vm((ROWS, DH), F32), vm((ROWS, DH), F32), vm((ROWS, DH), F32),
            vm((8, 3, MID, DH), F32), vm((3, MID, DH), F32),
            pltpu.SemaphoreType.DMA((64,)), pltpu.SemaphoreType.DMA((64,)),
            pltpu.SemaphoreType.DMA((24,)),
        ],
        cost_estimate=pl.CostEstimate(flops=15_000_000_000, bytes_accessed=24_000_000, transcendentals=8_000_000),
        compiler_params=pltpu.CompilerParams(
            collective_id=0, has_side_effects=True, vmem_limit_bytes=56 * 2 ** 20),
    )(queries, keys, values, w_out)


def solution(mesh):
    placed = (P("ctx", "head"), P("ctx", "head"), P("ctx", "head"), P("head", None))
    return jax.shard_map(
        local, mesh=mesh, in_specs=placed, out_specs=P("ctx", "head"), check_vma=False
    )
```

```python
import math

import jax
import jax.numpy as jnp
from jax import lax
from jax.experimental import pallas as pl
from jax.experimental.pallas import tpu as pltpu
from jax.sharding import PartitionSpec as P

MESH = pl.DeviceIdType.MESH
DH = 128
HEADS_HERE = 8
ROWS = 1024
COLS = 1024
MID = 128
TOP = 32
R_MID = 8
R_TOP = 32
QB = 256
NEG = -1e30
COEF = DH ** -0.5 / math.log(2.0)
F32 = jnp.float32
BF16 = jnp.bfloat16


def dot_t(a, b):
    return lax.dot_general(a, b, (((1,), (1,)), ((), ())), preferred_element_type=F32)


def dot(a, b):
    return jnp.dot(a, b, preferred_element_type=F32)


class Ring:
    def __init__(self, copy, plus, minus, own, far_plus, far_minus):
        self.first = [copy(*own[0], plus), copy(*own[1], minus)]
        self.second = [copy(*far_plus, plus), copy(*far_minus, minus)]

    def start(self):
        for one in self.first:
            one.start()

    def forward(self):
        for came, onward in zip(self.first, self.second):
            came.wait_recv()
            onward.start()

    def finish(self):
        for one in self.second:
            one.wait_recv()

    def drain(self):
        for one in self.first + self.second:
            one.wait_send()


def attend(qs, parts):
    scores = []
    for key, _, ok in parts:
        one = dot_t(qs, key)
        scores.append(one if ok is None else jnp.where(ok, one, NEG))
    peak = jnp.max(scores[0], axis=1, keepdims=True)
    for one in scores[1:]:
        peak = jnp.maximum(peak, jnp.max(one, axis=1, keepdims=True))
    acc = None
    for one, (_, val, _) in zip(scores, parts):
        term = dot(jnp.exp2((one - peak) * COEF).astype(BF16), val)
        acc = term if acc is None else acc + term
    total = acc[:, DH:]
    return acc[:, :DH] / total, jnp.broadcast_to(peak * COEF, total.shape) + jnp.log2(total)


def with_ones(val):
    return jnp.concatenate([val, jnp.ones(val.shape, BF16)], axis=1)


def body(q_hbm, k_hbm, v_hbm, w_hbm, out_hbm,
         q, k, v, wc_own, wo_own, attn, attn_p, wc, wo, rs_s, rs_r, out,
         patch, patch_p, st_mid, st_top, mid, top, res_mid, res_top, ret_mid, ret_top,
         wide, e0, o0, aff, spread, send, recv, lsem):
    place = lax.axis_index("ctx")
    h = lax.axis_index("head")
    z = lax.div(place, 8)
    x = lax.rem(lax.div(place, 2), 4)
    c = lax.rem(place, 2)
    s = x * 2 + c
    u = z * 2 + c
    near = h + 1 - 2 * lax.rem(h, 2)
    pair = (1 - c) * near + c * (3 - h)
    cross = c * near + (1 - c) * (3 - h)
    diag = lax.rem(h + 2, 4)

    def at(zz, xx, cc):
        return lax.rem(zz, 4) * 8 + lax.rem(xx, 4) * 2 + cc

    xp, xm = (at(z, x + 1, c), h), (at(z, x + 3, c), h)
    zp, zm = (at(z + 1, x, c), h), (at(z + 3, x, c), h)
    dp, dc = (place, pair), (place, cross)
    row_mates = [lax.rem(s + d, 8) for d in range(1, 8)]
    row_devs = [(z * 8 + t, h) for t in row_mates]
    col_mates = [lax.rem(u + d, 8) for d in range(1, 8)]
    col_devs = [(at(lax.div(t, 2), x, lax.rem(t, 2)), h) for t in col_mates]

    count = [0]

    def copy(src, dst, device):
        i = count[0]
        count[0] += 1
        return pltpu.make_async_remote_copy(
            src_ref=src, dst_ref=dst, send_sem=send.at[i], recv_sem=recv.at[i],
            device_id=device, device_id_type=MESH)

    lcount = [0]

    def load(src, dst):
        i = lcount[0]
        lcount[0] += 1
        return pltpu.make_async_copy(src, dst, lsem.at[i])

    xl, xr = lax.rem(x + 3, 4), lax.rem(x + 1, 4)

    loads = [load(q_hbm, q), load(k_hbm, k), load(v_hbm, v)]
    for one in loads:
        one.start()

    barrier = pltpu.get_barrier_semaphore()
    for other in row_devs + [(at(z + d, x, cc), h) for d in (1, 2, 3) for cc in (0, 1)] + [dp, dc]:
        pl.semaphore_signal(barrier, inc=1, device_id=other, device_id_type=MESH)

    w_loads = []
    for d in range(4):
        zc = lax.rem(z + d, 4) * 256
        for block, dst in ((cross, wc_own), (h, wo_own)):
            w_loads.append(load(w_hbm.at[:, pl.ds(pl.multiple_of(block * COLS + zc, 256), 256)], dst.at[d]))

    def pick(j, carry):
        cols = pl.ds(pl.multiple_of(j * DH, DH), DH)
        for i, src in enumerate((q, k, v)):
            wide[...] = src[:, cols].astype(F32)
            st_mid[j, i] = wide[pl.ds(j, MID, stride=R_MID), :].astype(BF16)
            st_top[j, i] = wide[pl.ds(h * 8 + j, TOP, stride=R_TOP), :].astype(BF16)
        return carry

    for one in loads:
        one.wait()
    lax.fori_loop(0, HEADS_HERE, pick, 0)
    mid[s] = st_mid[s]
    top[x, :, u] = st_top[u]
    pl.semaphore_wait(barrier, 15)

    mid_go = [copy(st_mid.at[t], mid.at[s], one) for t, one in zip(row_mates, row_devs)]
    top_go = [copy(st_top.at[t], top.at[x, :, u], one) for t, one in zip(col_mates, col_devs)]
    mid_back = [copy(res_mid.at[t], ret_mid.at[s], one) for t, one in zip(row_mates, row_devs)]
    top_back = [copy(res_top.at[t], ret_top.at[u], one) for t, one in zip(col_mates, col_devs)]

    def w_piece(block):
        return w_hbm.at[pl.ds(pl.multiple_of(x * 256, 256), 256),
                        pl.ds(pl.multiple_of(block * COLS + z * 256, 256), 256)]

    wc_hop = copy(w_piece(diag), wc.at[0, x], dp)
    wo_hop = copy(w_piece(pair), wo.at[x, 0], dp)
    top_x = Ring(copy, xp, xm,
                 [(top.at[x, pl.ds(1, 2)], top.at[x, pl.ds(1, 2)])] * 2,
                 (top.at[xl, 1], top.at[xl, 1]),
                 (top.at[xr, 2], top.at[xr, 2]))
    wc_x = Ring(copy, xp, xm,
                [(wc.at[0, x], wc.at[0, x])] * 2,
                (wc.at[0, xl, pl.ds(0, 128)], wc.at[0, xl, pl.ds(0, 128)]),
                (wc.at[0, xr, pl.ds(128, 128)], wc.at[0, xr, pl.ds(128, 128)]))
    wc_z = Ring(copy, zp, zm,
                [(wc.at[0], wc.at[3]), (wc.at[0], wc.at[1])],
                (wc.at[3, pl.ds(0, 2)], wc.at[2, pl.ds(0, 2)]),
                (wc.at[1, pl.ds(2, 2)], wc.at[2, pl.ds(2, 2)]))
    wo_z = Ring(copy, zp, zm,
                [(wo.at[x, 0], wo.at[x, 3]), (wo.at[x, 0], wo.at[x, 1])],
                (wo.at[x, 3, pl.ds(0, 128)], wo.at[x, 2, pl.ds(0, 128)]),
                (wo.at[x, 1, pl.ds(128, 128)], wo.at[x, 2, pl.ds(128, 128)]))
    wo_x = Ring(copy, xp, xm,
                [(wo.at[x], wo.at[x])] * 2,
                (wo.at[xl, pl.ds(0, 2)], wo.at[xl, pl.ds(0, 2)]),
                (wo.at[xr, pl.ds(2, 2)], wo.at[xr, pl.ds(2, 2)]))

    for one in top_go + mid_go + [wc_hop, wo_hop]:
        one.start()
    for one in w_loads:
        one.start()

    base = count[0]
    count[0] += HEADS_HERE
    tri = lax.broadcasted_iota(jnp.int32, (QB, QB), 0) >= lax.broadcasted_iota(jnp.int32, (QB, QB), 1)

    def attn_send(j):
        cols = pl.ds(pl.multiple_of(j * DH, DH), DH)
        return pltpu.make_async_remote_copy(
            src_ref=attn.at[:, cols], dst_ref=attn_p.at[:, cols],
            send_sem=send.at[base + j], recv_sem=recv.at[base + j],
            device_id=dp, device_id_type=MESH)

    def level0(j, carry):
        cols = pl.ds(pl.multiple_of(j * DH, DH), DH)
        vx = with_ones(v[:, cols])
        for i in range(ROWS // QB):
            here, past = pl.ds(i * QB, QB), pl.ds(0, i * QB)
            parts = [(k[here, cols], vx[i * QB:(i + 1) * QB], tri)]
            if i:
                parts.append((k[past, cols], vx[:i * QB], None))
            o, e = attend(q[here, cols], parts)
            o0[here] = o
            e0[here] = e
            attn[here, cols] = o.astype(BF16)
        picked = pl.ds(j, MID, stride=R_MID)
        aff[j, 0] = o0[picked, :]
        aff[j, 1] = e0[picked, :]
        attn_send(j).start()
        return carry

    def level1():
        for i in range(4):
            now = mid[2 * i:2 * i + 2]
            parts = [(now[:, 1].reshape(QB, DH), with_ones(now[:, 2].reshape(QB, DH)), tri)]
            if i:
                past = mid[0:2 * i]
                parts.append((past[:, 1].reshape(i * QB, DH), with_ones(past[:, 2].reshape(i * QB, DH)), None))
            o, e = attend(now[:, 0].reshape(QB, DH), parts)
            for half in range(2):
                res_mid[2 * i + half, pl.ds(0, MID)] = o[half * MID:(half + 1) * MID]
                res_mid[2 * i + half, pl.ds(MID, 8)] = e[half * MID:(half + 1) * MID].T[:8]

    def level2():
        row = lax.broadcasted_iota(jnp.int32, (256, 1024), 0)
        col = lax.broadcasted_iota(jnp.int32, (256, 1024), 1)

        def spot(index, xx):
            return (((index >> 6) & 3) * 8 + xx * 2 + ((index >> 5) & 1)) * TOP + (index & 31)

        ok = spot(col, col >> 8) <= spot(row, x)
        key = top[:, 1].reshape(1024, DH)
        val = top[:, 2].reshape(1024, DH)
        o, e = attend(top[x, 0].reshape(256, DH), [(key, with_ones(val), ok)])
        for t in range(8):
            res_top[t, 0] = o[t * TOP:(t + 1) * TOP]
            res_top[t, 1] = e[t * TOP:(t + 1) * TOP]

    lax.fori_loop(0, 2, level0, 0)
    wc_hop.wait_recv()
    wo_hop.wait_recv()
    wc_x.start()
    wo_z.start()
    for one in top_go:
        one.wait_recv()
    top_x.start()
    lax.fori_loop(2, 4, level0, 0)
    for one in mid_go:
        one.wait_recv()
    level1()
    for one in mid_back:
        one.start()
    ret_mid[s] = res_mid[s]
    top_x.forward()
    wc_x.forward()
    wo_z.forward()
    lax.fori_loop(4, 6, level0, 0)
    wc_x.finish()
    wc_z.start()
    wo_z.finish()
    wo_x.start()
    top_x.finish()
    level2()
    for one in top_back:
        one.start()
    ret_top[u] = res_top[u]
    lax.fori_loop(6, 8, level0, 0)

    for one in mid_back + top_back:
        one.wait_recv()

    def late(j, carry):
        spread[0] = jnp.zeros((MID, DH), F32)
        spread[1] = jnp.full((MID, DH), NEG, F32)
        hit = pl.ds(h, TOP, stride=4)
        spread[0, hit, :] = ret_top[j, 0]
        spread[1, hit, :] = ret_top[j, 1]
        ea, et = aff[j, 1], spread[1]
        em = jnp.broadcast_to(ret_mid[j, pl.ds(MID, 1)], (MID, DH)).T
        peak = jnp.maximum(ea, jnp.maximum(em, et))
        fa, fm, ft = jnp.exp2(ea - peak), jnp.exp2(em - peak), jnp.exp2(et - peak)
        upper = aff[j, 0] * fa + ret_mid[j, pl.ds(0, MID)] * fm + spread[0] * ft
        patch[j] = (upper / (fa + fm + ft)).astype(BF16)
        return carry

    lax.fori_loop(0, HEADS_HERE, late, 0)
    patch_send = copy(patch, patch_p, dp)
    patch_send.start()

    def mend(target, source):
        def one(j, carry):
            cols = pl.ds(pl.multiple_of(j * DH, DH), DH)
            old = target[:, cols].astype(F32).reshape(MID, R_MID, DH)
            new = source[j].astype(F32).reshape(MID, 1, DH)
            lane = lax.broadcasted_iota(jnp.int32, (MID, R_MID, DH), 1)
            target[:, cols] = jnp.where(lane == j, new, old).reshape(ROWS, DH).astype(BF16)
            return carry
        lax.fori_loop(0, HEADS_HERE, one, 0)

    wc_z.forward()
    wo_x.forward()
    for j in range(HEADS_HERE):
        attn_send(j).wait_send()
    mend(attn, patch)
    for j in range(HEADS_HERE):
        attn_send(j).wait_recv()
    patch_send.wait_recv()
    mend(attn_p, patch_p)

    for one in w_loads:
        one.wait()
    HALF = ROWS // 2
    sums = []
    for d in (0, 1, 3, 2):
        if d == 2:
            wc_z.finish()
        for part in range(2):
            here = pl.ds(part * HALF, HALF)
            rs_s[d, here] = (dot(attn[here], wc_own[d])
                             + dot(attn_p[here], wc[d].reshape(1024, 256))).astype(BF16)
            one = copy(rs_s.at[d, here], rs_r.at[d, here], dc)
            one.start()
            sums.append((d, here, one))
    wo_x.finish()
    stores = []
    for d, here, one in sums:
        mine = dot(attn[here], wo_own[d]) + dot(attn_p[here], wo[:, d].reshape(1024, 256))
        one.wait_recv()
        out[d, here] = (mine + rs_r[d, here].astype(F32)).astype(BF16)
        zc = pl.multiple_of(lax.rem(z + d, 4) * 256, 256)
        stores.append(load(out.at[d, here], out_hbm.at[here, pl.ds(zc, 256)]))
        stores[-1].start()

    for ring in (wc_x, wc_z, wo_z, wo_x, top_x):
        ring.drain()
    for one in mid_go + top_go + mid_back + top_back + [wc_hop, wo_hop, patch_send] + [t[2] for t in sums]:
        one.wait_send()
    for one in stores:
        one.wait()


def local(queries, keys, values, w_out):
    any_space = pl.BlockSpec(memory_space=pl.ANY)
    vm = pltpu.VMEM
    return pl.pallas_call(
        body,
        name="attend",
        out_shape=jax.ShapeDtypeStruct((ROWS, COLS), BF16),
        in_specs=[any_space] * 4,
        out_specs=any_space,
        scratch_shapes=[
            vm((ROWS, COLS), BF16), vm((ROWS, COLS), BF16), vm((ROWS, COLS), BF16),
            vm((4, 1024, 256), BF16), vm((4, 1024, 256), BF16),
            vm((ROWS, COLS), BF16), vm((ROWS, COLS), BF16),
            vm((4, 4, 256, 256), BF16), vm((4, 4, 256, 256), BF16),
            vm((4, ROWS, 256), BF16), vm((4, ROWS, 256), BF16), vm((4, ROWS, 256), BF16),
            vm((8, MID, DH), BF16), vm((8, MID, DH), BF16),
            vm((8, 3, MID, DH), BF16), vm((8, 3, TOP, DH), BF16),
            vm((8, 3, MID, DH), BF16), vm((4, 3, 8, TOP, DH), BF16),
            vm((8, MID + 8, DH), F32), vm((8, 2, TOP, DH), F32),
            vm((8, MID + 8, DH), F32), vm((8, 2, TOP, DH), F32),
            vm((ROWS, DH), F32), vm((ROWS, DH), F32), vm((ROWS, DH), F32),
            vm((8, 2, MID, DH), F32), vm((2, MID, DH), F32),
            pltpu.SemaphoreType.DMA((80,)), pltpu.SemaphoreType.DMA((80,)),
            pltpu.SemaphoreType.DMA((24,)),
        ],
        cost_estimate=pl.CostEstimate(flops=15_000_000_000, bytes_accessed=24_000_000, transcendentals=8_000_000),
        compiler_params=pltpu.CompilerParams(
            collective_id=0, has_side_effects=True, vmem_limit_bytes=56 * 2 ** 20),
    )(queries, keys, values, w_out)


def solution(mesh):
    placed = (P("ctx", "head"), P("ctx", "head"), P("ctx", "head"), P("head", None))
    return jax.shard_map(
        local, mesh=mesh, in_specs=placed, out_specs=P("ctx", "head"), check_vma=False
    )
```

```python
import math

import jax
import jax.numpy as jnp
from jax import lax
from jax.experimental import pallas as pl
from jax.experimental.pallas import tpu as pltpu
from jax.sharding import PartitionSpec as P

MESH = pl.DeviceIdType.MESH
DH = 128
HEADS_HERE = 8
ROWS = 1024
COLS = 1024
MID = 128
TOP = 32
R_MID = 8
R_TOP = 32
QB = 256
NEG = -1e30
COEF = DH ** -0.5 / math.log(2.0)
F32 = jnp.float32
BF16 = jnp.bfloat16


def dot_t(a, b):
    return lax.dot_general(a, b, (((1,), (1,)), ((), ())), preferred_element_type=F32)


def dot(a, b):
    return jnp.dot(a, b, preferred_element_type=F32)


class Ring:
    def __init__(self, copy, plus, minus, own, far_plus, far_minus):
        self.first = [copy(*own[0], plus), copy(*own[1], minus)]
        self.second = [copy(*far_plus, plus), copy(*far_minus, minus)]

    def start(self):
        for one in self.first:
            one.start()

    def forward(self):
        for came, onward in zip(self.first, self.second):
            came.wait_recv()
            onward.start()

    def finish(self):
        for one in self.second:
            one.wait_recv()

    def drain(self):
        for one in self.first + self.second:
            one.wait_send()


def attend(qs, parts):
    scores = []
    for key, _, ok in parts:
        one = dot_t(qs, key)
        scores.append(one if ok is None else jnp.where(ok, one, NEG))
    peak = jnp.max(scores[0], axis=1, keepdims=True)
    for one in scores[1:]:
        peak = jnp.maximum(peak, jnp.max(one, axis=1, keepdims=True))
    acc = None
    for one, (_, val, _) in zip(scores, parts):
        term = dot(jnp.exp2((one - peak) * COEF).astype(BF16), val)
        acc = term if acc is None else acc + term
    total = acc[:, DH:]
    return acc[:, :DH] / total, jnp.broadcast_to(peak * COEF, total.shape) + jnp.log2(total)


def with_ones(val):
    return jnp.concatenate([val, jnp.ones(val.shape, BF16)], axis=1)


def body(q_hbm, k_hbm, v_hbm, w_hbm, out_hbm,
         q, k, v, wc_own, wo_own, attn, attn_p, wc, wo, rs_s, rs_r, out,
         st_mid, st_top, mid, top, res_mid, res_top, ret_mid, ret_top,
         wide, e0, o0, aff, spread, sums_f, send, recv, lsem):
    place = lax.axis_index("ctx")
    h = lax.axis_index("head")
    z = lax.div(place, 8)
    x = lax.rem(lax.div(place, 2), 4)
    c = lax.rem(place, 2)
    s = x * 2 + c
    u = z * 2 + c
    near = h + 1 - 2 * lax.rem(h, 2)
    pair = (1 - c) * near + c * (3 - h)
    cross = c * near + (1 - c) * (3 - h)
    diag = lax.rem(h + 2, 4)

    def at(zz, xx, cc):
        return lax.rem(zz, 4) * 8 + lax.rem(xx, 4) * 2 + cc

    xp, xm = (at(z, x + 1, c), h), (at(z, x + 3, c), h)
    zp, zm = (at(z + 1, x, c), h), (at(z + 3, x, c), h)
    dp, dc = (place, pair), (place, cross)
    row_mates = [lax.rem(s + d, 8) for d in range(1, 8)]
    row_devs = [(z * 8 + t, h) for t in row_mates]
    col_mates = [lax.rem(u + d, 8) for d in range(1, 8)]
    col_devs = [(at(lax.div(t, 2), x, lax.rem(t, 2)), h) for t in col_mates]

    count = [0]

    def copy(src, dst, device):
        i = count[0]
        count[0] += 1
        return pltpu.make_async_remote_copy(
            src_ref=src, dst_ref=dst, send_sem=send.at[i], recv_sem=recv.at[i],
            device_id=device, device_id_type=MESH)

    lcount = [0]

    def load(src, dst):
        i = lcount[0]
        lcount[0] += 1
        return pltpu.make_async_copy(src, dst, lsem.at[i])

    xl, xr = lax.rem(x + 3, 4), lax.rem(x + 1, 4)

    loads = [load(q_hbm, q), load(k_hbm, k), load(v_hbm, v)]
    for one in loads:
        one.start()

    barrier = pltpu.get_barrier_semaphore()
    for other in row_devs + [(at(z + d, x, cc), h) for d in (1, 2, 3) for cc in (0, 1)] + [dp, dc]:
        pl.semaphore_signal(barrier, inc=1, device_id=other, device_id_type=MESH)

    w_loads = []
    for d in range(4):
        zc = lax.rem(z + d, 4) * 256
        for block, dst in ((cross, wc_own), (h, wo_own)):
            w_loads.append(load(w_hbm.at[:, pl.ds(pl.multiple_of(block * COLS + zc, 256), 256)], dst.at[d]))

    def pick(j, carry):
        cols = pl.ds(pl.multiple_of(j * DH, DH), DH)
        for i, src in enumerate((q, k, v)):
            wide[...] = src[:, cols].astype(F32)
            st_mid[j, i] = wide[pl.ds(j, MID, stride=R_MID), :].astype(BF16)
            st_top[j, i] = wide[pl.ds(h * 8 + j, TOP, stride=R_TOP), :].astype(BF16)
        return carry

    for one in loads:
        one.wait()
    lax.fori_loop(0, HEADS_HERE, pick, 0)
    mid[s] = st_mid[s]
    top[x, :, u] = st_top[u]
    pl.semaphore_wait(barrier, 15)

    mid_go = [copy(st_mid.at[t], mid.at[s], one) for t, one in zip(row_mates, row_devs)]
    top_go = [copy(st_top.at[t], top.at[x, :, u], one) for t, one in zip(col_mates, col_devs)]
    mid_back = [copy(res_mid.at[t], ret_mid.at[s], one) for t, one in zip(row_mates, row_devs)]
    top_back = [copy(res_top.at[t], ret_top.at[u], one) for t, one in zip(col_mates, col_devs)]

    def w_piece(block):
        return w_hbm.at[pl.ds(pl.multiple_of(x * 256, 256), 256),
                        pl.ds(pl.multiple_of(block * COLS + z * 256, 256), 256)]

    wc_hop = copy(w_piece(diag), wc.at[0, x], dp)
    wo_hop = copy(w_piece(pair), wo.at[x, 0], dp)
    top_x = Ring(copy, xp, xm,
                 [(top.at[x, pl.ds(1, 2)], top.at[x, pl.ds(1, 2)])] * 2,
                 (top.at[xl, 1], top.at[xl, 1]),
                 (top.at[xr, 2], top.at[xr, 2]))
    wc_x = Ring(copy, xp, xm,
                [(wc.at[0, x], wc.at[0, x])] * 2,
                (wc.at[0, xl, pl.ds(0, 128)], wc.at[0, xl, pl.ds(0, 128)]),
                (wc.at[0, xr, pl.ds(128, 128)], wc.at[0, xr, pl.ds(128, 128)]))
    wc_z = Ring(copy, zp, zm,
                [(wc.at[0], wc.at[3]), (wc.at[0], wc.at[1])],
                (wc.at[3, pl.ds(0, 2)], wc.at[2, pl.ds(0, 2)]),
                (wc.at[1, pl.ds(2, 2)], wc.at[2, pl.ds(2, 2)]))
    wo_z = Ring(copy, zp, zm,
                [(wo.at[x, 0], wo.at[x, 3]), (wo.at[x, 0], wo.at[x, 1])],
                (wo.at[x, 3, pl.ds(0, 128)], wo.at[x, 2, pl.ds(0, 128)]),
                (wo.at[x, 1, pl.ds(128, 128)], wo.at[x, 2, pl.ds(128, 128)]))
    wo_x = Ring(copy, xp, xm,
                [(wo.at[x], wo.at[x])] * 2,
                (wo.at[xl, pl.ds(0, 2)], wo.at[xl, pl.ds(0, 2)]),
                (wo.at[xr, pl.ds(2, 2)], wo.at[xr, pl.ds(2, 2)]))

    for one in top_go + mid_go + [wc_hop, wo_hop]:
        one.start()
    for one in w_loads:
        one.start()

    base = count[0]
    count[0] += HEADS_HERE * R_MID
    tri = lax.broadcasted_iota(jnp.int32, (QB, QB), 0) >= lax.broadcasted_iota(jnp.int32, (QB, QB), 1)

    def attn_send(j, r):
        spot = (pl.ds(pl.multiple_of(r * MID, MID), MID), pl.ds(pl.multiple_of(j * DH, DH), DH))
        return pltpu.make_async_remote_copy(
            src_ref=attn.at[spot], dst_ref=attn_p.at[spot],
            send_sem=send.at[base + j * R_MID + r], recv_sem=recv.at[base + j * R_MID + r],
            device_id=dp, device_id_type=MESH)

    def level0(j, carry):
        cols = pl.ds(pl.multiple_of(j * DH, DH), DH)
        vx = with_ones(v[:, cols])
        for i in range(ROWS // QB):
            here, past = pl.ds(i * QB, QB), pl.ds(0, i * QB)
            parts = [(k[here, cols], vx[i * QB:(i + 1) * QB], tri)]
            if i:
                parts.append((k[past, cols], vx[:i * QB], None))
            o, e = attend(q[here, cols], parts)
            o0[here] = o
            e0[here] = e
        for r in range(R_MID):
            attn[pl.ds(r * MID, MID), cols] = o0[pl.ds(r, MID, stride=R_MID), :].astype(BF16)

        def leave(d, carry):
            attn_send(j, lax.rem(j + d, R_MID)).start()
            return carry

        lax.fori_loop(1, R_MID, leave, 0)
        picked = pl.ds(j, MID, stride=R_MID)
        aff[j, 0] = o0[picked, :]
        aff[j, 1] = e0[picked, :]
        return carry

    def level1():
        for i in range(4):
            now = mid[2 * i:2 * i + 2]
            parts = [(now[:, 1].reshape(QB, DH), with_ones(now[:, 2].reshape(QB, DH)), tri)]
            if i:
                past = mid[0:2 * i]
                parts.append((past[:, 1].reshape(i * QB, DH), with_ones(past[:, 2].reshape(i * QB, DH)), None))
            o, e = attend(now[:, 0].reshape(QB, DH), parts)
            for half in range(2):
                res_mid[2 * i + half, pl.ds(0, MID)] = o[half * MID:(half + 1) * MID].astype(BF16)
                rest = e[half * MID:(half + 1) * MID].T[:16]
                for n in range(3):
                    piece = rest.astype(BF16)
                    res_mid[2 * i + half, pl.ds(MID + 16 * n, 16)] = piece
                    rest = rest - piece.astype(F32)

    def level2():
        row = lax.broadcasted_iota(jnp.int32, (256, 1024), 0)
        col = lax.broadcasted_iota(jnp.int32, (256, 1024), 1)

        def spot(index, xx):
            return (((index >> 6) & 3) * 8 + xx * 2 + ((index >> 5) & 1)) * TOP + (index & 31)

        ok = spot(col, col >> 8) <= spot(row, x)
        key = top[:, 1].reshape(1024, DH)
        val = top[:, 2].reshape(1024, DH)
        o, e = attend(top[x, 0].reshape(256, DH), [(key, with_ones(val), ok)])
        for t in range(8):
            res_top[t, 0] = o[t * TOP:(t + 1) * TOP]
            res_top[t, 1] = e[t * TOP:(t + 1) * TOP]

    lax.fori_loop(0, 2, level0, 0)
    for one in top_go:
        one.wait_recv()
    top_x.start()
    wo_hop.wait_recv()
    wo_z.start()
    lax.fori_loop(2, 4, level0, 0)
    for one in mid_go:
        one.wait_recv()
    level1()
    for one in mid_back:
        one.start()
    ret_mid[s] = res_mid[s]
    top_x.forward()
    wc_hop.wait_recv()
    wc_x.start()
    lax.fori_loop(4, 6, level0, 0)
    top_x.finish()
    level2()
    for one in top_back:
        one.start()
    ret_top[u] = res_top[u]
    wc_x.forward()
    wo_z.forward()
    lax.fori_loop(6, 8, level0, 0)
    wc_x.finish()
    wc_z.start()

    for one in mid_back + top_back:
        one.wait_recv()
    wo_z.finish()
    wo_x.start()

    def late(j, carry):
        spread[0] = jnp.zeros((MID, DH), F32)
        spread[1] = jnp.full((MID, DH), NEG, F32)
        hit = pl.ds(h, TOP, stride=4)
        spread[0, hit, :] = ret_top[j, 0]
        spread[1, hit, :] = ret_top[j, 1]
        ea, et = aff[j, 1], spread[1]
        tail = [ret_mid[j, pl.ds(MID + 16 * n, 16)].astype(F32)[:1] for n in range(3)]
        em = jnp.broadcast_to(tail[0] + tail[1] + tail[2], (MID, DH)).T
        peak = jnp.maximum(ea, jnp.maximum(em, et))
        fa, fm, ft = jnp.exp2(ea - peak), jnp.exp2(em - peak), jnp.exp2(et - peak)
        upper = aff[j, 0] * fa + ret_mid[j, pl.ds(0, MID)].astype(F32) * fm + spread[0] * ft
        attn[pl.ds(pl.multiple_of(j * MID, MID), MID), pl.ds(pl.multiple_of(j * DH, DH), DH)] = (
            upper / (fa + fm + ft)).astype(BF16)
        attn_send(j, j).start()
        return carry

    lax.fori_loop(0, HEADS_HERE, late, 0)

    def came(n, carry):
        attn_send(lax.div(n, R_MID), lax.rem(n, R_MID)).wait_recv()
        return carry

    lax.fori_loop(0, HEADS_HERE * R_MID, came, 0)

    for one in w_loads:
        one.wait()
    HALF = ROWS // 2
    sums = []
    for d in (0, 1, 3, 2):
        if d == 1:
            wc_z.forward()
            wo_x.forward()
        if d == 2:
            wc_z.finish()
        for part in range(2):
            here = pl.ds(part * HALF, HALF)
            rs_s[d, here] = (dot(attn[here], wc_own[d])
                             + dot(attn_p[here], wc[d].reshape(1024, 256))).astype(BF16)
            one = copy(rs_s.at[d, here], rs_r.at[d, here], dc)
            one.start()
            sums.append((d, part, one))
    wo_x.finish()
    stores = []
    for d, part, one in sums:
        here = pl.ds(part * HALF, HALF)
        mine = dot(attn[here], wo_own[d]) + dot(attn_p[here], wo[:, d].reshape(1024, 256))
        one.wait_recv()
        both = mine + rs_r[d, here].astype(F32)
        for n in range(4):
            for lane in range(2):
                sums_f[lane, pl.ds(part * 4 + n, MID, stride=R_MID), :] = both[n * MID:(n + 1) * MID,
                                                                            lane * DH:(lane + 1) * DH]
        if part:
            for lane in range(2):
                out[d, :, lane * DH:(lane + 1) * DH] = sums_f[lane].astype(BF16)
            zc = pl.multiple_of(lax.rem(z + d, 4) * 256, 256)
            stores.append(load(out.at[d], out_hbm.at[:, pl.ds(zc, 256)]))
            stores[-1].start()

    for ring in (wc_x, wc_z, wo_z, wo_x, top_x):
        ring.drain()
    for one in mid_go + top_go + mid_back + top_back + [wc_hop, wo_hop] + [t[2] for t in sums]:
        one.wait_send()

    def gone(n, carry):
        attn_send(lax.div(n, R_MID), lax.rem(n, R_MID)).wait_send()
        return carry

    lax.fori_loop(0, HEADS_HERE * R_MID, gone, 0)
    for one in stores:
        one.wait()


def local(queries, keys, values, w_out):
    any_space = pl.BlockSpec(memory_space=pl.ANY)
    vm = pltpu.VMEM
    return pl.pallas_call(
        body,
        name="attend",
        out_shape=jax.ShapeDtypeStruct((ROWS, COLS), BF16),
        in_specs=[any_space] * 4,
        out_specs=any_space,
        scratch_shapes=[
            vm((ROWS, COLS), BF16), vm((ROWS, COLS), BF16), vm((ROWS, COLS), BF16),
            vm((4, 1024, 256), BF16), vm((4, 1024, 256), BF16),
            vm((ROWS, COLS), BF16), vm((ROWS, COLS), BF16),
            vm((4, 4, 256, 256), BF16), vm((4, 4, 256, 256), BF16),
            vm((4, ROWS, 256), BF16), vm((4, ROWS, 256), BF16), vm((4, ROWS, 256), BF16),
            vm((8, 3, MID, DH), BF16), vm((8, 3, TOP, DH), BF16),
            vm((8, 3, MID, DH), BF16), vm((4, 3, 8, TOP, DH), BF16),
            vm((8, MID + 48, DH), BF16), vm((8, 2, TOP, DH), F32),
            vm((8, MID + 48, DH), BF16), vm((8, 2, TOP, DH), F32),
            vm((ROWS, DH), F32), vm((ROWS, DH), F32), vm((ROWS, DH), F32),
            vm((8, 2, MID, DH), F32), vm((2, MID, DH), F32),
            vm((2, ROWS, DH), F32),
            pltpu.SemaphoreType.DMA((144,)), pltpu.SemaphoreType.DMA((144,)),
            pltpu.SemaphoreType.DMA((24,)),
        ],
        cost_estimate=pl.CostEstimate(flops=15_000_000_000, bytes_accessed=24_000_000, transcendentals=8_000_000),
        compiler_params=pltpu.CompilerParams(
            collective_id=0, has_side_effects=True, vmem_limit_bytes=56 * 2 ** 20),
    )(queries, keys, values, w_out)


def solution(mesh):
    placed = (P("ctx", "head"), P("ctx", "head"), P("ctx", "head"), P("head", None))
    return jax.shard_map(
        local, mesh=mesh, in_specs=placed, out_specs=P("ctx", "head"), check_vma=False
    )
```

```python
import math

import jax
import jax.numpy as jnp
from jax import lax
from jax.experimental import pallas as pl
from jax.experimental.pallas import tpu as pltpu
from jax.sharding import PartitionSpec as P

MESH = pl.DeviceIdType.MESH
DH = 128
HEADS_HERE = 8
ROWS = 1024
COLS = 1024
MID = 128
TOP = 32
R_MID = 8
R_TOP = 32
QB = 256
NEG = -1e30
COEF = DH ** -0.5 / math.log(2.0)
F32 = jnp.float32
BF16 = jnp.bfloat16


def dot_t(a, b):
    return lax.dot_general(a, b, (((1,), (1,)), ((), ())), preferred_element_type=F32)


def dot(a, b):
    return jnp.dot(a, b, preferred_element_type=F32)


class Ring:
    def __init__(self, copy, plus, minus, own, far_plus, far_minus):
        self.first = [copy(*own[0], plus), copy(*own[1], minus)]
        self.second = [copy(*far_plus, plus), copy(*far_minus, minus)]

    def start(self):
        for one in self.first:
            one.start()

    def forward(self):
        for came, onward in zip(self.first, self.second):
            came.wait_recv()
            onward.start()

    def finish(self):
        for one in self.second:
            one.wait_recv()

    def drain(self):
        for one in self.first + self.second:
            one.wait_send()


def attend(qs, parts):
    scores = []
    for key, _, ok in parts:
        one = dot_t(qs, key)
        scores.append(one if ok is None else jnp.where(ok, one, NEG))
    peak = jnp.max(scores[0], axis=1, keepdims=True)
    for one in scores[1:]:
        peak = jnp.maximum(peak, jnp.max(one, axis=1, keepdims=True))
    acc = None
    for one, (_, val, _) in zip(scores, parts):
        term = dot(jnp.exp2((one - peak) * COEF).astype(BF16), val)
        acc = term if acc is None else acc + term
    total = acc[:, DH:]
    return acc[:, :DH] / total, jnp.broadcast_to(peak * COEF, total.shape) + jnp.log2(total)


def with_ones(val):
    return jnp.concatenate([val, jnp.ones(val.shape, BF16)], axis=1)


def body(q_hbm, k_hbm, v_hbm, w_hbm, out_hbm,
         q, k, v, wc_own, wo_own, attn, attn_p, wc, wo, rs_s, rs_r, out,
         st_mid, st_top, mid, top, res_mid, ret_mid,
         wide, e0, o0, aff, extra, sums_f, send, recv, lsem):
    place = lax.axis_index("ctx")
    h = lax.axis_index("head")
    z = lax.div(place, 8)
    x = lax.rem(lax.div(place, 2), 4)
    c = lax.rem(place, 2)
    s = x * 2 + c
    near = h + 1 - 2 * lax.rem(h, 2)
    pair = (1 - c) * near + c * (3 - h)
    cross = c * near + (1 - c) * (3 - h)
    diag = lax.rem(h + 2, 4)

    def at(zz, xx, cc):
        return lax.rem(zz, 4) * 8 + lax.rem(xx, 4) * 2 + cc

    xp, xm = (at(z, x + 1, c), h), (at(z, x + 3, c), h)
    zp, zm = (at(z + 1, x, c), h), (at(z + 3, x, c), h)
    dp, dc = (place, pair), (place, cross)
    row_mates = [lax.rem(s + d, 8) for d in range(1, 8)]
    row_devs = [(z * 8 + t, h) for t in row_mates]

    count = [0]

    def copy(src, dst, device):
        i = count[0]
        count[0] += 1
        return pltpu.make_async_remote_copy(
            src_ref=src, dst_ref=dst, send_sem=send.at[i], recv_sem=recv.at[i],
            device_id=device, device_id_type=MESH)

    lcount = [0]

    def load(src, dst):
        i = lcount[0]
        lcount[0] += 1
        return pltpu.make_async_copy(src, dst, lsem.at[i])

    xl, xr = lax.rem(x + 3, 4), lax.rem(x + 1, 4)
    zl, zr = lax.rem(z + 3, 4), lax.rem(z + 1, 4)

    loads = [load(q_hbm, q), load(k_hbm, k), load(v_hbm, v)]
    for one in loads:
        one.start()

    barrier = pltpu.get_barrier_semaphore()
    for other in row_devs + [zp, zm, dp, dc]:
        pl.semaphore_signal(barrier, inc=1, device_id=other, device_id_type=MESH)

    w_loads = []
    for d in range(4):
        zc = lax.rem(z + d, 4) * 256
        for block, dst in ((cross, wc_own), (h, wo_own)):
            w_loads.append(load(w_hbm.at[:, pl.ds(pl.multiple_of(block * COLS + zc, 256), 256)], dst.at[d]))

    def pick(j, carry):
        cols = pl.ds(pl.multiple_of(j * DH, DH), DH)
        for i, src in enumerate((q, k, v)):
            wide[...] = src[:, cols].astype(F32)
            st_mid[j, i] = wide[pl.ds(j, MID, stride=R_MID), :].astype(BF16)
            st_top[j, i] = wide[pl.ds(h * 8 + j, TOP, stride=R_TOP), :].astype(BF16)
        return carry

    for one in loads:
        one.wait()
    lax.fori_loop(0, HEADS_HERE, pick, 0)
    mid[s] = st_mid[s]
    top[z, :, s] = st_top[s]
    extra[0] = jnp.zeros((ROWS, DH), F32)
    extra[1] = jnp.full((ROWS, DH), NEG, F32)
    pl.semaphore_wait(barrier, 11)

    mid_go = [copy(st_mid.at[t], mid.at[s], one) for t, one in zip(row_mates, row_devs)]
    top_go = [copy(st_top.at[t], top.at[z, :, s], one) for t, one in zip(row_mates, row_devs)]
    mid_back = [copy(res_mid.at[t], ret_mid.at[s], one) for t, one in zip(row_mates, row_devs)]

    def w_piece(block, n, d):
        return w_hbm.at[pl.ds(pl.multiple_of(n * 256, 256), 256),
                        pl.ds(pl.multiple_of(block * COLS + lax.rem(z + d, 4) * 256, 256), 256)]

    wc_hop = [copy(w_piece(diag, n, 0), wc.at[0, n], dp) for n in range(4)]
    wo_hop = [copy(w_piece(pair, x, d), wo.at[x, d], dp) for d in range(4)]
    top_z = Ring(copy, zp, zm,
                 [(top.at[z, pl.ds(1, 2)], top.at[z, pl.ds(1, 2)])] * 2,
                 (top.at[zl, 1], top.at[zl, 1]),
                 (top.at[zr, 2], top.at[zr, 2]))
    wc_z = Ring(copy, zp, zm,
                [(wc.at[0], wc.at[3]), (wc.at[0], wc.at[1])],
                (wc.at[3, pl.ds(0, 2)], wc.at[2, pl.ds(0, 2)]),
                (wc.at[1, pl.ds(2, 2)], wc.at[2, pl.ds(2, 2)]))
    wo_x = Ring(copy, xp, xm,
                [(wo.at[x], wo.at[x])] * 2,
                (wo.at[xl, pl.ds(0, 2)], wo.at[xl, pl.ds(0, 2)]),
                (wo.at[xr, pl.ds(2, 2)], wo.at[xr, pl.ds(2, 2)]))

    for one in top_go + mid_go + wc_hop + wo_hop:
        one.start()
    for one in w_loads:
        one.start()

    base = count[0]
    count[0] += HEADS_HERE * R_MID
    tri = lax.broadcasted_iota(jnp.int32, (QB, QB), 0) >= lax.broadcasted_iota(jnp.int32, (QB, QB), 1)

    def attn_send(j, r):
        spot = (pl.ds(pl.multiple_of(r * MID, MID), MID), pl.ds(pl.multiple_of(j * DH, DH), DH))
        return pltpu.make_async_remote_copy(
            src_ref=attn.at[spot], dst_ref=attn_p.at[spot],
            send_sem=send.at[base + j * R_MID + r], recv_sem=recv.at[base + j * R_MID + r],
            device_id=dp, device_id_type=MESH)

    def level0(j, carry):
        cols = pl.ds(pl.multiple_of(j * DH, DH), DH)
        vx = with_ones(v[:, cols])
        for i in range(ROWS // QB):
            here, past = pl.ds(i * QB, QB), pl.ds(0, i * QB)
            parts = [(k[here, cols], vx[i * QB:(i + 1) * QB], tri)]
            if i:
                parts.append((k[past, cols], vx[:i * QB], None))
            o, e = attend(q[here, cols], parts)
            o0[here] = o
            e0[here] = e
        for r in range(R_MID):
            attn[pl.ds(r * MID, MID), cols] = o0[pl.ds(r, MID, stride=R_MID), :].astype(BF16)

        def leave(d, carry):
            attn_send(j, lax.rem(j + d, R_MID)).start()
            return carry

        lax.fori_loop(1, R_MID, leave, 0)
        picked = pl.ds(j, MID, stride=R_MID)
        aff[j, 0] = o0[picked, :]
        aff[j, 1] = e0[picked, :]
        return carry

    def level1():
        for i in range(4):
            now = mid[2 * i:2 * i + 2]
            parts = [(now[:, 1].reshape(QB, DH), with_ones(now[:, 2].reshape(QB, DH)), tri)]
            if i:
                past = mid[0:2 * i]
                parts.append((past[:, 1].reshape(i * QB, DH), with_ones(past[:, 2].reshape(i * QB, DH)), None))
            o, e = attend(now[:, 0].reshape(QB, DH), parts)
            here = pl.ds(i * QB, QB)
            et = extra[1, here]
            peak = jnp.maximum(e, et)
            fm, ft = jnp.exp2(e - peak), jnp.exp2(et - peak)
            both = fm + ft
            o = (o * fm + extra[0, here] * ft) / both
            e = peak + jnp.log2(both)
            for half in range(2):
                res_mid[2 * i + half, pl.ds(0, MID)] = o[half * MID:(half + 1) * MID].astype(BF16)
                rest = e[half * MID:(half + 1) * MID].T[:16]
                for n in range(3):
                    piece = rest.astype(BF16)
                    res_mid[2 * i + half, pl.ds(MID + 16 * n, 16)] = piece
                    rest = rest - piece.astype(F32)

    def level2():
        row = lax.broadcasted_iota(jnp.int32, (256, 1024), 0)
        col = lax.broadcasted_iota(jnp.int32, (256, 1024), 1)
        key = top[:, 1].reshape(1024, DH)
        val = top[:, 2].reshape(1024, DH)
        o, e = attend(top[z, 0].reshape(256, DH), [(key, with_ones(val), col <= row + z * 256)])
        hit = pl.ds(h, 256, stride=4)
        extra[0, hit, :] = o
        extra[1, hit, :] = e

    lax.fori_loop(0, 2, level0, 0)
    for one in top_go:
        one.wait_recv()
    top_z.start()
    lax.fori_loop(2, 4, level0, 0)
    top_z.forward()
    for one in wc_hop:
        one.wait_recv()
    wc_z.start()
    lax.fori_loop(4, 6, level0, 0)
    top_z.finish()
    level2()
    for one in mid_go:
        one.wait_recv()
    level1()
    for one in mid_back:
        one.start()
    ret_mid[s] = res_mid[s]
    for one in wo_hop:
        one.wait_recv()
    wo_x.start()
    lax.fori_loop(6, 8, level0, 0)

    for one in mid_back:
        one.wait_recv()

    def late(j, carry):
        ea = aff[j, 1]
        tail = [ret_mid[j, pl.ds(MID + 16 * n, 16)].astype(F32)[:1] for n in range(3)]
        em = jnp.broadcast_to(tail[0] + tail[1] + tail[2], (MID, DH)).T
        peak = jnp.maximum(ea, em)
        fa, fm = jnp.exp2(ea - peak), jnp.exp2(em - peak)
        upper = aff[j, 0] * fa + ret_mid[j, pl.ds(0, MID)].astype(F32) * fm
        attn[pl.ds(pl.multiple_of(j * MID, MID), MID), pl.ds(pl.multiple_of(j * DH, DH), DH)] = (
            upper / (fa + fm)).astype(BF16)
        attn_send(j, j).start()
        return carry

    lax.fori_loop(0, HEADS_HERE, late, 0)
    wc_z.forward()

    def came(n, carry):
        attn_send(lax.div(n, R_MID), lax.rem(n, R_MID)).wait_recv()
        return carry

    lax.fori_loop(0, HEADS_HERE * R_MID, came, 0)

    for one in w_loads:
        one.wait()
    HALF = ROWS // 2
    sums = []
    for d in (0, 1, 3, 2):
        if d == 1:
            wo_x.forward()
        if d == 2:
            wc_z.finish()
        for part in range(2):
            here = pl.ds(part * HALF, HALF)
            rs_s[d, here] = (dot(attn[here], wc_own[d])
                             + dot(attn_p[here], wc[d].reshape(1024, 256))).astype(BF16)
            one = copy(rs_s.at[d, here], rs_r.at[d, here], dc)
            one.start()
            sums.append((d, part, one))
    wo_x.finish()
    stores = []
    for d, part, one in sums:
        here = pl.ds(part * HALF, HALF)
        mine = dot(attn[here], wo_own[d]) + dot(attn_p[here], wo[:, d].reshape(1024, 256))
        one.wait_recv()
        both = mine + rs_r[d, here].astype(F32)
        for n in range(4):
            for lane in range(2):
                sums_f[lane, pl.ds(part * 4 + n, MID, stride=R_MID), :] = both[n * MID:(n + 1) * MID,
                                                                            lane * DH:(lane + 1) * DH]
        if part:
            for lane in range(2):
                out[d, :, lane * DH:(lane + 1) * DH] = sums_f[lane].astype(BF16)
            zc = pl.multiple_of(lax.rem(z + d, 4) * 256, 256)
            stores.append(load(out.at[d], out_hbm.at[:, pl.ds(zc, 256)]))
            stores[-1].start()

    for ring in (wc_z, wo_x, top_z):
        ring.drain()
    for one in mid_go + top_go + mid_back + wo_hop + wc_hop + [t[2] for t in sums]:
        one.wait_send()

    def gone(n, carry):
        attn_send(lax.div(n, R_MID), lax.rem(n, R_MID)).wait_send()
        return carry

    lax.fori_loop(0, HEADS_HERE * R_MID, gone, 0)
    for one in stores:
        one.wait()


def local(queries, keys, values, w_out):
    any_space = pl.BlockSpec(memory_space=pl.ANY)
    vm = pltpu.VMEM
    return pl.pallas_call(
        body,
        name="attend",
        out_shape=jax.ShapeDtypeStruct((ROWS, COLS), BF16),
        in_specs=[any_space] * 4,
        out_specs=any_space,
        scratch_shapes=[
            vm((ROWS, COLS), BF16), vm((ROWS, COLS), BF16), vm((ROWS, COLS), BF16),
            vm((4, 1024, 256), BF16), vm((4, 1024, 256), BF16),
            vm((ROWS, COLS), BF16), vm((ROWS, COLS), BF16),
            vm((4, 4, 256, 256), BF16), vm((4, 4, 256, 256), BF16),
            vm((4, ROWS, 256), BF16), vm((4, ROWS, 256), BF16), vm((4, ROWS, 256), BF16),
            vm((8, 3, MID, DH), BF16), vm((8, 3, TOP, DH), BF16),
            vm((8, 3, MID, DH), BF16), vm((4, 3, 8, TOP, DH), BF16),
            vm((8, MID + 48, DH), BF16), vm((8, MID + 48, DH), BF16),
            vm((ROWS, DH), F32), vm((ROWS, DH), F32), vm((ROWS, DH), F32),
            vm((8, 2, MID, DH), F32), vm((2, ROWS, DH), F32),
            vm((2, ROWS, DH), F32),
            pltpu.SemaphoreType.DMA((144,)), pltpu.SemaphoreType.DMA((144,)),
            pltpu.SemaphoreType.DMA((24,)),
        ],
        cost_estimate=pl.CostEstimate(flops=15_000_000_000, bytes_accessed=24_000_000, transcendentals=8_000_000),
        compiler_params=pltpu.CompilerParams(
            collective_id=0, has_side_effects=True, vmem_limit_bytes=56 * 2 ** 20),
    )(queries, keys, values, w_out)


def solution(mesh):
    placed = (P("ctx", "head"), P("ctx", "head"), P("ctx", "head"), P("head", None))
    return jax.shard_map(
        local, mesh=mesh, in_specs=placed, out_specs=P("ctx", "head"), check_vma=False
    )
```

```python
import math

import jax
import jax.numpy as jnp
from jax import lax
from jax.experimental import pallas as pl
from jax.experimental.pallas import tpu as pltpu
from jax.sharding import PartitionSpec as P

MESH = pl.DeviceIdType.MESH
DH = 128
HEADS_HERE = 8
ROWS = 1024
COLS = 1024
MID = 128
TOP = 32
R_MID = 8
R_TOP = 32
QB = 256
NEG = -1e30
COEF = DH ** -0.5 / math.log(2.0)
F32 = jnp.float32
BF16 = jnp.bfloat16


def dot_t(a, b):
    return lax.dot_general(a, b, (((1,), (1,)), ((), ())), preferred_element_type=F32)


def dot(a, b):
    return jnp.dot(a, b, preferred_element_type=F32)


class Ring:
    def __init__(self, copy, plus, minus, own, far_plus, far_minus):
        self.first = [copy(*own[0], plus), copy(*own[1], minus)]
        self.second = [copy(*far_plus, plus), copy(*far_minus, minus)]

    def start(self):
        for one in self.first:
            one.start()

    def forward(self):
        for came, onward in zip(self.first, self.second):
            came.wait_recv()
            onward.start()

    def finish(self):
        for one in self.second:
            one.wait_recv()

    def drain(self):
        for one in self.first + self.second:
            one.wait_send()


def attend(qs, parts):
    scores = []
    for key, _, ok in parts:
        one = dot_t(qs, key)
        scores.append(one if ok is None else jnp.where(ok, one, NEG))
    peak = jnp.max(scores[0], axis=1, keepdims=True)
    for one in scores[1:]:
        peak = jnp.maximum(peak, jnp.max(one, axis=1, keepdims=True))
    acc = None
    for one, (_, val, _) in zip(scores, parts):
        term = dot(jnp.exp2((one - peak) * COEF).astype(BF16), val)
        acc = term if acc is None else acc + term
    total = acc[:, DH:]
    return acc[:, :DH] / total, jnp.broadcast_to(peak * COEF, total.shape) + jnp.log2(total)


def with_ones(val):
    return jnp.concatenate([val, jnp.ones(val.shape, BF16)], axis=1)


def body(q_hbm, k_hbm, v_hbm, w_hbm, out_hbm,
         q, k, v, wc_own, wo_own, attn, attn_p, wc, wo, rs_s, rs_r, out,
         st_mid, st_top, mid, top, res_mid, ret_mid,
         wide, e0, o0, aff, extra, sums_f, send, recv, lsem):
    place = lax.axis_index("ctx")
    h = lax.axis_index("head")
    z = lax.div(place, 8)
    x = lax.rem(lax.div(place, 2), 4)
    c = lax.rem(place, 2)
    s = x * 2 + c
    near = h + 1 - 2 * lax.rem(h, 2)
    pair = (1 - c) * near + c * (3 - h)
    cross = c * near + (1 - c) * (3 - h)
    diag = lax.rem(h + 2, 4)

    def at(zz, xx, cc):
        return lax.rem(zz, 4) * 8 + lax.rem(xx, 4) * 2 + cc

    xp, xm = (at(z, x + 1, c), h), (at(z, x + 3, c), h)
    zp, zm = (at(z + 1, x, c), h), (at(z + 3, x, c), h)
    dp, dc = (place, pair), (place, cross)
    row_mates = [lax.rem(s + d, 8) for d in range(1, 8)]
    row_devs = [(z * 8 + t, h) for t in row_mates]

    count = [0]

    def copy(src, dst, device):
        i = count[0]
        count[0] += 1
        return pltpu.make_async_remote_copy(
            src_ref=src, dst_ref=dst, send_sem=send.at[i], recv_sem=recv.at[i],
            device_id=device, device_id_type=MESH)

    lcount = [0]

    def load(src, dst):
        i = lcount[0]
        lcount[0] += 1
        return pltpu.make_async_copy(src, dst, lsem.at[i])

    xl, xr = lax.rem(x + 3, 4), lax.rem(x + 1, 4)
    zl, zr = lax.rem(z + 3, 4), lax.rem(z + 1, 4)

    loads = [load(q_hbm, q), load(k_hbm, k), load(v_hbm, v)]
    for one in loads:
        one.start()

    barrier = pltpu.get_barrier_semaphore()
    for other in row_devs + [zp, zm, dp, dc]:
        pl.semaphore_signal(barrier, inc=1, device_id=other, device_id_type=MESH)

    w_loads = []
    for d in range(4):
        zc = lax.rem(z + d, 4) * 256
        for block, dst in ((cross, wc_own), (h, wo_own)):
            w_loads.append(load(w_hbm.at[:, pl.ds(pl.multiple_of(block * COLS + zc, 256), 256)], dst.at[d]))

    def pick(j, carry):
        cols = pl.ds(pl.multiple_of(j * DH, DH), DH)
        for i, src in enumerate((q, k, v)):
            wide[...] = src[:, cols].astype(F32)
            st_mid[j, i] = wide[pl.ds(j, MID, stride=R_MID), :].astype(BF16)
            st_top[j, i] = wide[pl.ds(h * 8 + j, TOP, stride=R_TOP), :].astype(BF16)
        return carry

    for one in loads:
        one.wait()
    lax.fori_loop(0, HEADS_HERE, pick, 0)
    mid[s] = st_mid[s]
    top[z, :, s] = st_top[s]
    extra[0] = jnp.zeros((ROWS, DH), F32)
    extra[1] = jnp.full((ROWS, DH), NEG, F32)
    pl.semaphore_wait(barrier, 11)

    mid_go = [copy(st_mid.at[t], mid.at[s], one) for t, one in zip(row_mates, row_devs)]
    top_go = [copy(st_top.at[t], top.at[z, :, s], one) for t, one in zip(row_mates, row_devs)]
    mid_back = [copy(res_mid.at[t], ret_mid.at[s], one) for t, one in zip(row_mates, row_devs)]

    def w_piece(block, n, d):
        return w_hbm.at[pl.ds(pl.multiple_of(n * 256, 256), 256),
                        pl.ds(pl.multiple_of(block * COLS + lax.rem(z + d, 4) * 256, 256), 256)]

    wc_hop = [copy(w_piece(diag, n, 0), wc.at[0, n], dp) for n in range(4)]
    wo_hop = [copy(w_piece(pair, x, d), wo.at[x, d], dp) for d in (0, 2)]
    wo_z = [copy(wo.at[x, 0], wo.at[x, 3], zp), copy(wo.at[x, 0], wo.at[x, 1], zm)]
    top_z = Ring(copy, zp, zm,
                 [(top.at[z, pl.ds(1, 2)], top.at[z, pl.ds(1, 2)])] * 2,
                 (top.at[zl, 1], top.at[zl, 1]),
                 (top.at[zr, 2], top.at[zr, 2]))
    wc_z = Ring(copy, zp, zm,
                [(wc.at[0], wc.at[3]), (wc.at[0], wc.at[1])],
                (wc.at[3, pl.ds(0, 2)], wc.at[2, pl.ds(0, 2)]),
                (wc.at[1, pl.ds(2, 2)], wc.at[2, pl.ds(2, 2)]))
    wo_x = Ring(copy, xp, xm,
                [(wo.at[x], wo.at[x])] * 2,
                (wo.at[xl, pl.ds(0, 2)], wo.at[xl, pl.ds(0, 2)]),
                (wo.at[xr, pl.ds(2, 2)], wo.at[xr, pl.ds(2, 2)]))

    for one in top_go + mid_go + wc_hop + wo_hop:
        one.start()
    for one in w_loads:
        one.start()

    base = count[0]
    count[0] += HEADS_HERE * R_MID
    tri = lax.broadcasted_iota(jnp.int32, (QB, QB), 0) >= lax.broadcasted_iota(jnp.int32, (QB, QB), 1)

    def attn_send(j, r):
        spot = (pl.ds(pl.multiple_of(r * MID, MID), MID), pl.ds(pl.multiple_of(j * DH, DH), DH))
        return pltpu.make_async_remote_copy(
            src_ref=attn.at[spot], dst_ref=attn_p.at[spot],
            send_sem=send.at[base + j * R_MID + r], recv_sem=recv.at[base + j * R_MID + r],
            device_id=dp, device_id_type=MESH)

    def level0(j, carry):
        cols = pl.ds(pl.multiple_of(j * DH, DH), DH)
        vx = with_ones(v[:, cols])
        for i in range(ROWS // QB):
            here, past = pl.ds(i * QB, QB), pl.ds(0, i * QB)
            parts = [(k[here, cols], vx[i * QB:(i + 1) * QB], tri)]
            if i:
                parts.append((k[past, cols], vx[:i * QB], None))
            o, e = attend(q[here, cols], parts)
            o0[here] = o
            e0[here] = e
        for r in range(R_MID):
            attn[pl.ds(r * MID, MID), cols] = o0[pl.ds(r, MID, stride=R_MID), :].astype(BF16)

        def leave(d, carry):
            attn_send(j, lax.rem(j + d, R_MID)).start()
            return carry

        lax.fori_loop(1, R_MID, leave, 0)
        picked = pl.ds(j, MID, stride=R_MID)
        aff[j, 0] = o0[picked, :]
        aff[j, 1] = e0[picked, :]
        return carry

    def level1():
        for i in range(4):
            now = mid[2 * i:2 * i + 2]
            parts = [(now[:, 1].reshape(QB, DH), with_ones(now[:, 2].reshape(QB, DH)), tri)]
            if i:
                past = mid[0:2 * i]
                parts.append((past[:, 1].reshape(i * QB, DH), with_ones(past[:, 2].reshape(i * QB, DH)), None))
            o, e = attend(now[:, 0].reshape(QB, DH), parts)
            here = pl.ds(i * QB, QB)
            et = extra[1, here]
            peak = jnp.maximum(e, et)
            fm, ft = jnp.exp2(e - peak), jnp.exp2(et - peak)
            both = fm + ft
            o = (o * fm + extra[0, here] * ft) / both
            e = peak + jnp.log2(both)
            for half in range(2):
                res_mid[2 * i + half, pl.ds(0, MID)] = o[half * MID:(half + 1) * MID].astype(BF16)
                rest = e[half * MID:(half + 1) * MID].T[:16]
                for n in range(3):
                    piece = rest.astype(BF16)
                    res_mid[2 * i + half, pl.ds(MID + 16 * n, 16)] = piece
                    rest = rest - piece.astype(F32)

    def level2():
        row = lax.broadcasted_iota(jnp.int32, (256, 1024), 0)
        col = lax.broadcasted_iota(jnp.int32, (256, 1024), 1)
        key = top[:, 1].reshape(1024, DH)
        val = top[:, 2].reshape(1024, DH)
        o, e = attend(top[z, 0].reshape(256, DH), [(key, with_ones(val), col <= row + z * 256)])
        hit = pl.ds(h, 256, stride=4)
        extra[0, hit, :] = o
        extra[1, hit, :] = e

    lax.fori_loop(0, 2, level0, 0)
    for one in top_go:
        one.wait_recv()
    top_z.start()
    lax.fori_loop(2, 4, level0, 0)
    top_z.forward()
    wo_hop[0].wait_recv()
    for one in wo_z:
        one.start()
    for one in wc_hop:
        one.wait_recv()
    wc_z.start()
    lax.fori_loop(4, 6, level0, 0)
    top_z.finish()
    level2()
    for one in mid_go:
        one.wait_recv()
    level1()
    for one in mid_back:
        one.start()
    ret_mid[s] = res_mid[s]
    for one in wo_hop[1:] + wo_z:
        one.wait_recv()
    wo_x.start()
    lax.fori_loop(6, 8, level0, 0)

    for one in mid_back:
        one.wait_recv()

    def late(j, carry):
        ea = aff[j, 1]
        tail = [ret_mid[j, pl.ds(MID + 16 * n, 16)].astype(F32)[:1] for n in range(3)]
        em = jnp.broadcast_to(tail[0] + tail[1] + tail[2], (MID, DH)).T
        peak = jnp.maximum(ea, em)
        fa, fm = jnp.exp2(ea - peak), jnp.exp2(em - peak)
        upper = aff[j, 0] * fa + ret_mid[j, pl.ds(0, MID)].astype(F32) * fm
        attn[pl.ds(pl.multiple_of(j * MID, MID), MID), pl.ds(pl.multiple_of(j * DH, DH), DH)] = (
            upper / (fa + fm)).astype(BF16)
        attn_send(j, j).start()
        return carry

    lax.fori_loop(0, HEADS_HERE, late, 0)
    wc_z.forward()

    def came(n, carry):
        attn_send(lax.div(n, R_MID), lax.rem(n, R_MID)).wait_recv()
        return carry

    lax.fori_loop(0, HEADS_HERE * R_MID, came, 0)

    for one in w_loads:
        one.wait()
    HALF = ROWS // 2
    sums = []
    for d in (0, 1, 3, 2):
        if d == 1:
            wo_x.forward()
        if d == 2:
            wc_z.finish()
        for part in range(2):
            here = pl.ds(part * HALF, HALF)
            rs_s[d, here] = (dot(attn[here], wc_own[d])
                             + dot(attn_p[here], wc[d].reshape(1024, 256))).astype(BF16)
            one = copy(rs_s.at[d, here], rs_r.at[d, here], dc)
            one.start()
            sums.append((d, part, one))
    wo_x.finish()
    stores = []
    for d, part, one in sums:
        here = pl.ds(part * HALF, HALF)
        mine = dot(attn[here], wo_own[d]) + dot(attn_p[here], wo[:, d].reshape(1024, 256))
        one.wait_recv()
        both = mine + rs_r[d, here].astype(F32)
        for n in range(4):
            for lane in range(2):
                sums_f[lane, pl.ds(part * 4 + n, MID, stride=R_MID), :] = both[n * MID:(n + 1) * MID,
                                                                            lane * DH:(lane + 1) * DH]
        if part:
            for lane in range(2):
                out[d, :, lane * DH:(lane + 1) * DH] = sums_f[lane].astype(BF16)
            zc = pl.multiple_of(lax.rem(z + d, 4) * 256, 256)
            stores.append(load(out.at[d], out_hbm.at[:, pl.ds(zc, 256)]))
            stores[-1].start()

    for ring in (wc_z, wo_x, top_z):
        ring.drain()
    for one in mid_go + top_go + mid_back + wo_hop + wo_z + wc_hop + [t[2] for t in sums]:
        one.wait_send()

    def gone(n, carry):
        attn_send(lax.div(n, R_MID), lax.rem(n, R_MID)).wait_send()
        return carry

    lax.fori_loop(0, HEADS_HERE * R_MID, gone, 0)
    for one in stores:
        one.wait()


def local(queries, keys, values, w_out):
    any_space = pl.BlockSpec(memory_space=pl.ANY)
    vm = pltpu.VMEM
    return pl.pallas_call(
        body,
        name="attend",
        out_shape=jax.ShapeDtypeStruct((ROWS, COLS), BF16),
        in_specs=[any_space] * 4,
        out_specs=any_space,
        scratch_shapes=[
            vm((ROWS, COLS), BF16), vm((ROWS, COLS), BF16), vm((ROWS, COLS), BF16),
            vm((4, 1024, 256), BF16), vm((4, 1024, 256), BF16),
            vm((ROWS, COLS), BF16), vm((ROWS, COLS), BF16),
            vm((4, 4, 256, 256), BF16), vm((4, 4, 256, 256), BF16),
            vm((4, ROWS, 256), BF16), vm((4, ROWS, 256), BF16), vm((4, ROWS, 256), BF16),
            vm((8, 3, MID, DH), BF16), vm((8, 3, TOP, DH), BF16),
            vm((8, 3, MID, DH), BF16), vm((4, 3, 8, TOP, DH), BF16),
            vm((8, MID + 48, DH), BF16), vm((8, MID + 48, DH), BF16),
            vm((ROWS, DH), F32), vm((ROWS, DH), F32), vm((ROWS, DH), F32),
            vm((8, 2, MID, DH), F32), vm((2, ROWS, DH), F32),
            vm((2, ROWS, DH), F32),
            pltpu.SemaphoreType.DMA((144,)), pltpu.SemaphoreType.DMA((144,)),
            pltpu.SemaphoreType.DMA((24,)),
        ],
        cost_estimate=pl.CostEstimate(flops=15_000_000_000, bytes_accessed=24_000_000, transcendentals=8_000_000),
        compiler_params=pltpu.CompilerParams(
            collective_id=0, has_side_effects=True, vmem_limit_bytes=56 * 2 ** 20),
    )(queries, keys, values, w_out)


def solution(mesh):
    placed = (P("ctx", "head"), P("ctx", "head"), P("ctx", "head"), P("head", None))
    return jax.shard_map(
        local, mesh=mesh, in_specs=placed, out_specs=P("ctx", "head"), check_vma=False
    )
```
